32 devices in a mesh: tm: 16 (over z, x, core), space: 2 (over y).
Axes of the slice: x: 2, y: 2, z: 4, core: 2. Of those that a mesh axis runs over, the one named last changes fastest.
Arguments:
- forcing: float32 [64, 8, 128, 128], P('tm', 'space'), may hold values from -6 to 6
- conductivity: float32 [8, 128, 128], P('space'), may hold values from 0.5 to 2
- guess: float32 [16, 8, 128, 128], P('tm', 'space'), may hold values from -6 to 6
Outputs:
- solution: float32 [64, 8, 128, 128], P('tm', 'space')
The draws below stay inside these ranges and needn't reach their ends.
All inputs are finite; a program needn't handle non-finite values.
Results may differ from the reference program's by a relative error of at most 0.00002.
Values sent between devices are 32-bit elements; how exact they have to be, the bound alone decides.
A program may use at most 64 MiB of HBM per device.

```python
import math
import jax
import jax.numpy as jnp

SX = 128
SY = 128
CF = 4
NT = 64
NZ = 8
NC = 16
N_TM = 16


def levels(stream_key, dims, split, low, largest):
    def one(position, blocks):
        steps = jax.random.uniform(jax.random.fold_in(jax.random.fold_in(stream_key, 6), position), (blocks,), jnp.float32, low / len(split), largest / len(split))
        return jnp.repeat(jnp.exp(steps), dims[position] // blocks).reshape((-1,) + (1,) * (len(dims) - position - 1))

    gain = one(*split[0])
    for cut in split[1:]:
        gain = gain * one(*cut)
    return gain


def gaussian(key, extent, spread, reach, shards=(), kind=jnp.bfloat16):
    entries = jax.random.normal(key, extent, jnp.float32) * spread
    if len(shards) > 0:
        entries = levels(key, extent, shards, -0.22, 0.18) * entries
    return jnp.clip(entries, min=-reach, max=reach).astype(kind)


def setup_inputs(seed: int = 0) -> dict:
    streams_of = jax.random.split(jax.random.key(seed), 4)
    forcing = gaussian(streams_of[0], (NT, NZ, SX, SY), 1.0, 6.0, ((0, 16), (1, 2)), jnp.float32)
    conductivity = jnp.clip(jnp.exp(math.log(2.0) - 1.3862944 * jax.random.uniform(streams_of[1], (NZ, SX, SY), jnp.float32) ** levels(streams_of[1], (NZ, SX, SY), ((0, 2),), -0.2, 0.2)), 0.5, 2.0)
    guess = gaussian(streams_of[2], (NC, NZ, SX, SY), 1.0, 6.0, ((0, 16), (1, 2)), jnp.float32)
    return dict(forcing=forcing, conductivity=conductivity, guess=guess)


step_length = 0.1


def neighbours(field):
    padded = jnp.pad(field, ((0, 0), (1, 1), (0, 0), (0, 0)))
    total = padded[:, :-2] + padded[:, 2:]
    total = total + jnp.roll(field, 1, axis=2) + jnp.roll(field, -1, axis=2)
    return total + jnp.roll(field, 1, axis=3) + jnp.roll(field, -1, axis=3)


def two_sweeps(start, target, weight, scaled):
    first = (target + weight * neighbours(start)) / scaled
    return (target + weight * neighbours(first)) / scaled


def reference(forcing, conductivity, guess):
    kappa = conductivity[None]
    fine_weight = step_length * kappa
    fine_scaled = 1.0 + 6.0 * fine_weight
    coarse_weight = CF * step_length * kappa
    coarse_scaled = 1.0 + 6.0 * coarse_weight
    sources = forcing.reshape(N_TM, CF, NZ, SX, SY)

    def fine_step(state, source):
        return two_sweeps(state, state + step_length * source, fine_weight, fine_scaled)

    def relax(anchor):
        states = [anchor]
        for index in range(1, CF):
            states.append(fine_step(states[-1], sources[:, index]))
        return jnp.stack(states, axis=1)

    anchor = guess
    states = relax(anchor)
    before = jnp.roll(states[:, CF - 1], 1, axis=0)
    defect = fine_step(before, sources[:, 0]) - anchor
    total = defect
    for turn in range(N_TM - 1):
        moved = jnp.roll(total, 1, axis=0)
        total = defect + two_sweeps(moved, moved, coarse_weight, coarse_scaled)
    anchor = anchor + total
    return relax(anchor).reshape(NT, NZ, SX, SY)
```

```python
import functools

import jax
import jax.numpy as jnp
from jax import lax
from jax.experimental import pallas as pl
from jax.experimental.pallas import tpu as pltpu
from jax.sharding import PartitionSpec as P

step_length = 0.1
MESH = pl.DeviceIdType.MESH
SUB = 8


def kernel(nt, ns, cf, zl, sx, forcing, kappa_in, guess_in, out,
           kap, gue, src, cur, mid, tot, bef, anc, slots, tgt, wf, wc, stage,
           loc_sem, send_sem, recv_sem, tm_send, tm_recv, an_send, an_recv, out_sem):
    rows = sx // SUB
    nz = ns * zl
    k = lax.axis_index("tm")
    h = lax.axis_index("space")
    owner = lax.rem(k, ns)
    active = h == owner
    shifts = []
    step = 1
    while step < nt:
        shifts.append(step)
        step *= 2
    offsets = sorted({o % nt for s in shifts for o in (s, -s)} - {0})

    barrier = pltpu.get_barrier_semaphore()
    for d in range(1, ns):
        pl.semaphore_signal(barrier, inc=1, device_id=(k, lax.rem(h + d, ns)), device_id_type=MESH)

    @pl.when(active)
    def _():
        for o in offsets:
            kk = lax.rem(k + o, nt)
            pl.semaphore_signal(barrier, inc=1, device_id=(kk, lax.rem(kk, ns)), device_id_type=MESH)

    own = pl.ds(h * zl, zl)
    local = [pltpu.make_async_copy(kappa_in, kap.at[own], loc_sem.at[0]),
             pltpu.make_async_copy(guess_in.at[0], gue.at[own], loc_sem.at[1])]
    for j in range(cf):
        local.append(pltpu.make_async_copy(forcing.at[j], src.at[j, own], loc_sem.at[2 + j]))
    for copy in local:
        copy.start()

    @pl.when(active)
    def _():
        pl.semaphore_wait(barrier, ns - 1 + len(offsets))

    @pl.when(jnp.logical_not(active))
    def _():
        pl.semaphore_wait(barrier, ns - 1)

    def piece(a, d, sender, target):
        planes = pl.ds(sender * zl, zl)
        if a == 0:
            s, t = kappa_in, kap.at[planes]
        elif a == 1:
            s, t = guess_in.at[0], gue.at[planes]
        else:
            s, t = forcing.at[a - 2], src.at[a - 2, planes]
        return pltpu.make_async_remote_copy(
            src_ref=s, dst_ref=t, send_sem=send_sem.at[a, d], recv_sem=recv_sem.at[a, d],
            device_id=(k, target), device_id_type=MESH)

    first = [0, 1] + [2 + j for j in range(1, cf)] + [2]
    second = [0] + [2 + j for j in range(1, cf)]

    def send_first():
        for d in range(1, ns):
            target = lax.rem(h + d, ns)

            @pl.when(target == owner)
            def _():
                for a in first:
                    piece(a, d, h, target).start()

    def send_second():
        for d in range(1, ns):
            target = lax.rem(h + d, ns)

            @pl.when(target != owner)
            def _():
                for a in second:
                    piece(a, d, h, target).start()

    def arrive(a):
        for d in range(1, ns):
            piece(a, d, lax.rem(h + ns - d, ns), h).wait_recv()

    def planes_loop(body):
        lax.fori_loop(0, nz, lambda z, c: (body(z), c)[1], 0)

    def natural(ref, z, r):
        return ref[z, pl.ds(r, SUB, stride=rows), :]

    def sums(f, z):
        c = [f[z + 1, r] for r in range(rows)]
        res = []
        for r in range(rows):
            lo = c[r - 1] if r > 0 else pltpu.roll(c[rows - 1], 1, 0)
            hi = c[r + 1] if r < rows - 1 else pltpu.roll(c[0], SUB - 1, 0)
            n = (f[z, r] + f[z + 2, r]) + (lo + hi)
            width = c[r].shape[1]
            res.append(n + (pltpu.roll(c[r], 1, 1) + pltpu.roll(c[r], width - 1, 1)))
        return c, res

    def step_of(f, w, source):
        def one(z):
            c, n = sums(f, z)
            for r in range(rows):
                wr = w[z, r]
                b = c[r]
                if source is not None:
                    b = b + step_length * natural(source, z, r)
                t = b - (6.0 * wr) * b
                tgt[z, r] = t
                mid[z + 1, r] = t + wr * n[r]

        def two(z):
            _, n = sums(mid, z)
            for r in range(rows):
                f[z + 1, r] = tgt[z, r] + w[z, r] * n[r]

        planes_loop(one)
        planes_loop(two)

    def zero_ends(ref):
        zero = jnp.zeros(ref.shape[1:], jnp.float32)
        ref[0] = zero
        ref[nz + 1] = zero

    def weights():
        def body(z):
            for r in range(rows):
                kp = natural(kap, z, r)
                a = step_length * kp
                wf[z, r] = a / (1.0 + 6.0 * a)
                b = (cf * step_length) * kp
                wc[z, r] = b / (1.0 + 6.0 * b)
        planes_loop(body)

    def shift(i, s, source, target):
        kk = lax.rem(k + s, nt)
        return pltpu.make_async_remote_copy(
            src_ref=source.at[pl.ds(1, nz)], dst_ref=target.at[pl.ds(1, nz)],
            send_sem=tm_send.at[i], recv_sem=tm_recv.at[i],
            device_id=(kk, lax.rem(kk, ns)), device_id_type=MESH)

    def anchor_copy(d, target):
        return pltpu.make_async_remote_copy(
            src_ref=anc.at[pl.ds(1, nz)], dst_ref=anc.at[pl.ds(1, nz)],
            send_sem=an_send.at[d], recv_sem=an_recv.at[d],
            device_id=(k, target), device_id_type=MESH)

    send_first()

    @pl.when(jnp.logical_not(active))
    def _():
        send_second()

    zero_ends(mid)
    zero_ends(anc)
    for copy in local:
        copy.wait()

    @pl.when(active)
    def _():
        zero_ends(cur)
        zero_ends(bef)
        for i in range(len(shifts)):
            zero_ends(slots.at[i])
        arrive(0)
        weights()
        arrive(1)

        def load(z):
            for r in range(rows):
                cur[z + 1, r] = natural(gue, z, r)

        planes_loop(load)
        for j in range(1, cf):
            arrive(2 + j)
            step_of(cur, wf, src.at[j])
        move = shift(0, 1, cur, bef)
        move.start()
        arrive(2)
        move.wait()
        step_of(bef, wf, src.at[0])

        def defect(z):
            for r in range(rows):
                tot[z + 1, r] = bef[z + 1, r] - natural(gue, z, r)

        planes_loop(defect)
        for i, s in enumerate(shifts):
            slot = slots.at[i]
            move = shift(1 + i, s, tot, slot)
            move.start()
            move.wait_recv()
            if i == 0:
                send_second()

            def again(n, c):
                step_of(slot, wc, None)
                return c

            lax.fori_loop(0, s, again, 0)
            move.wait_send()
            last = i == len(shifts) - 1

            def add(z):
                for r in range(rows):
                    v = tot[z + 1, r] + slot[z + 1, r]
                    if last:
                        anc[z + 1, r] = v + natural(gue, z, r)
                    else:
                        tot[z + 1, r] = v

            planes_loop(add)
        for d in range(1, ns):
            anchor_copy(d, lax.rem(h + d, ns)).start()

    @pl.when(jnp.logical_not(active))
    def _():
        for a in second:
            arrive(a)
        weights()
        for d in range(1, ns):
            @pl.when(lax.rem(h + ns - d, ns) == owner)
            def _():
                anchor_copy(d, h).wait_recv()

    @pl.when(active)
    def _():
        for d in range(1, ns):
            anchor_copy(d, lax.rem(h + d, ns)).wait_send()

    results = []
    for j in range(cf):
        if j > 0:
            step_of(anc, wf, src.at[j])

        def put(z, c):
            for r in range(rows):
                stage[j, z, pl.ds(r, SUB, stride=rows), :] = anc[h * zl + z + 1, r]
            return c

        lax.fori_loop(0, zl, put, 0)
        copy = pltpu.make_async_copy(stage.at[j], out.at[j], out_sem.at[j])
        copy.start()
        results.append(copy)
    for d in range(1, ns):
        target = lax.rem(h + d, ns)

        @pl.when(target == owner)
        def _():
            for a in first:
                piece(a, d, h, target).wait_send()

        @pl.when(target != owner)
        def _():
            for a in second:
                piece(a, d, h, target).wait_send()
    for copy in results:
        copy.wait()


def per_device(nt, ns, forcing, conductivity, guess):
    cf, zl, sx, sy = forcing.shape
    nz = zl * ns
    rows = sx // SUB
    hops = max(1, (nt - 1).bit_length())
    f32 = jnp.float32
    field = pltpu.VMEM((nz + 2, rows, SUB, sy), f32)
    inner = pltpu.VMEM((nz, rows, SUB, sy), f32)
    plain = pltpu.VMEM((nz, sx, sy), f32)
    dma = pltpu.SemaphoreType.DMA
    return pl.pallas_call(
        functools.partial(kernel, nt, ns, cf, zl, sx),
        out_shape=jax.ShapeDtypeStruct(forcing.shape, f32),
        in_specs=[pl.BlockSpec(memory_space=pl.ANY)] * 3,
        out_specs=pl.BlockSpec(memory_space=pl.ANY),
        scratch_shapes=[
            plain, plain, pltpu.VMEM((cf, nz, sx, sy), f32),
            field, field, field, field, field,
            pltpu.VMEM((hops, nz + 2, rows, SUB, sy), f32),
            inner, inner, inner,
            pltpu.VMEM((cf, zl, sx, sy), f32),
            dma((cf + 2,)), dma((cf + 2, ns)), dma((cf + 2, ns)),
            dma((hops + 1,)), dma((hops + 1,)), dma((ns,)), dma((ns,)), dma((cf,)),
        ],
        compiler_params=pltpu.CompilerParams(
            collective_id=0, has_side_effects=True, vmem_limit_bytes=56 * 1024 * 1024),
    )(forcing, conductivity, guess)


def solution(mesh):
    in_specs = (P("tm", "space", None, None), P("space", None, None), P("tm", "space", None, None))
    return jax.shard_map(
        functools.partial(per_device, mesh.shape["tm"], mesh.shape["space"]),
        mesh=mesh, in_specs=in_specs, out_specs=P("tm", "space", None, None), check_vma=False)
```

```python
import functools

import jax
import jax.numpy as jnp
from jax import lax
from jax.experimental import pallas as pl
from jax.experimental.pallas import tpu as pltpu
from jax.sharding import PartitionSpec as P

step_length = 0.1
MESH = pl.DeviceIdType.MESH
SUB = 8
UNROLL = 8
PARTS = 1


def kernel(nt, ns, cf, zl, sx, forcing, kappa_in, guess_in, out,
           kap, gue, src, cur, mid, tot, bef, anc, slots, tgt, wf, wc, stage,
           loc_sem, send_sem, recv_sem, tm_send, tm_recv, an_send, an_recv, out_sem):
    rows = sx // SUB
    nz = ns * zl
    k = lax.axis_index("tm")
    h = lax.axis_index("space")
    owner = lax.rem(k, ns)
    active = h == owner
    shifts = []
    step = 1
    while step < nt:
        shifts.append(step)
        step *= 2
    offsets = sorted({o % nt for s in shifts for o in (s, -s)} - {0})

    barrier = pltpu.get_barrier_semaphore()
    for d in range(1, ns):
        pl.semaphore_signal(barrier, inc=1, device_id=(k, lax.rem(h + d, ns)), device_id_type=MESH)

    @pl.when(active)
    def _():
        for o in offsets:
            kk = lax.rem(k + o, nt)
            pl.semaphore_signal(barrier, inc=1, device_id=(kk, lax.rem(kk, ns)), device_id_type=MESH)

    own = pl.ds(h * zl, zl)
    local = [pltpu.make_async_copy(kappa_in, kap.at[own], loc_sem.at[0]),
             pltpu.make_async_copy(guess_in.at[0], gue.at[own], loc_sem.at[1])]
    for j in range(cf):
        local.append(pltpu.make_async_copy(forcing.at[j], src.at[j, own], loc_sem.at[2 + j]))
    for copy in local:
        copy.start()

    @pl.when(active)
    def _():
        pl.semaphore_wait(barrier, ns - 1 + len(offsets))

    @pl.when(jnp.logical_not(active))
    def _():
        pl.semaphore_wait(barrier, ns - 1)

    def piece(a, d, sender, target):
        planes = pl.ds(sender * zl, zl)
        if a == 0:
            s, t = kappa_in, kap.at[planes]
        elif a == 1:
            s, t = guess_in.at[0], gue.at[planes]
        else:
            s, t = forcing.at[a - 2], src.at[a - 2, planes]
        return pltpu.make_async_remote_copy(
            src_ref=s, dst_ref=t, send_sem=send_sem.at[a, d], recv_sem=recv_sem.at[a, d],
            device_id=(k, target), device_id_type=MESH)

    first = [0, 1] + [2 + j for j in range(1, cf)] + [2]
    second = [0] + [2 + j for j in range(1, cf)]

    def send_first():
        for d in range(1, ns):
            target = lax.rem(h + d, ns)

            @pl.when(target == owner)
            def _():
                for n, a in enumerate(first):
                    if n > 1:
                        piece(first[n - 2], d, h, target).wait_send()
                    piece(a, d, h, target).start()

    def send_second():
        for d in range(1, ns):
            target = lax.rem(h + d, ns)

            @pl.when(target != owner)
            def _():
                for a in second:
                    piece(a, d, h, target).start()

    def arrive(a):
        for d in range(1, ns):
            piece(a, d, lax.rem(h + ns - d, ns), h).wait_recv()

    def planes_loop(body):
        def group(g, c):
            for u in range(UNROLL):
                body(g * UNROLL + u)
            return c

        if nz == UNROLL:
            group(0, 0)
        else:
            whole = nz // UNROLL
            lax.fori_loop(0, whole, group, 0)
            for z in range(whole * UNROLL, nz):
                body(z)

    def natural(ref, z, r):
        return ref[z, pl.ds(r, SUB, stride=rows), :]

    def total(f, z, r):
        c = f[z + 1, r]
        lo = f[z + 1, r - 1] if r > 0 else pltpu.roll(f[z + 1, rows - 1], 1, 0)
        hi = f[z + 1, r + 1] if r < rows - 1 else pltpu.roll(f[z + 1, 0], SUB - 1, 0)
        side = pltpu.roll(c, 1, 1) + pltpu.roll(c, c.shape[1] - 1, 1)
        return c, ((f[z, r] + f[z + 2, r]) + (lo + hi)) + side

    def step_of(f, w, source):
        def one(z):
            for r in range(rows):
                b, n = total(f, z, r)
                wr = w[z, r]
                if source is not None:
                    b = b + step_length * natural(source, z, r)
                t = b - (6.0 * wr) * b
                tgt[z, r] = t
                mid[z + 1, r] = t + wr * n

        def two(z):
            for r in range(rows):
                _, n = total(mid, z, r)
                f[z + 1, r] = tgt[z, r] + w[z, r] * n

        planes_loop(one)
        planes_loop(two)

    def zero_ends(ref):
        zero = jnp.zeros(ref.shape[1:], jnp.float32)
        ref[0] = zero
        ref[nz + 1] = zero

    def weights():
        def body(z):
            for r in range(rows):
                kp = natural(kap, z, r)
                a = step_length * kp
                wf[z, r] = a / (1.0 + 6.0 * a)
                b = (cf * step_length) * kp
                wc[z, r] = b / (1.0 + 6.0 * b)
        planes_loop(body)

    part = nz // PARTS

    def shift(i, s, source, target):
        kk = lax.rem(k + s, nt)
        return [pltpu.make_async_remote_copy(
            src_ref=source.at[pl.ds(1 + q * part, part)],
            dst_ref=target.at[pl.ds(1 + q * part, part)],
            send_sem=tm_send.at[i, q], recv_sem=tm_recv.at[i, q],
            device_id=(kk, lax.rem(kk, ns)), device_id_type=MESH) for q in range(PARTS)]

    def anchor_copy(d, target):
        return [pltpu.make_async_remote_copy(
            src_ref=anc.at[pl.ds(1 + q * part, part)],
            dst_ref=anc.at[pl.ds(1 + q * part, part)],
            send_sem=an_send.at[d, q], recv_sem=an_recv.at[d, q],
            device_id=(k, target), device_id_type=MESH) for q in range(PARTS)]

    def start(copies):
        for one in copies:
            one.start()

    def wait_recv(copies):
        for one in copies:
            one.wait_recv()

    def wait_send(copies):
        for one in copies:
            one.wait_send()

    send_first()

    @pl.when(jnp.logical_not(active))
    def _():
        send_second()

    zero_ends(mid)
    zero_ends(anc)
    for copy in local:
        copy.wait()

    @pl.when(active)
    def _():
        zero_ends(cur)
        zero_ends(bef)
        for i in range(len(shifts)):
            zero_ends(slots.at[i])
        arrive(0)
        weights()
        arrive(1)

        def load(z):
            for r in range(rows):
                cur[z + 1, r] = natural(gue, z, r)

        planes_loop(load)
        for j in range(1, cf):
            arrive(2 + j)
            step_of(cur, wf, src.at[j])
        move = shift(0, 1, cur, bef)
        start(move)
        arrive(2)
        wait_recv(move)
        wait_send(move)
        step_of(bef, wf, src.at[0])

        def defect(z):
            for r in range(rows):
                tot[z + 1, r] = bef[z + 1, r] - natural(gue, z, r)

        planes_loop(defect)
        for i, s in enumerate(shifts):
            slot = slots.at[i]
            move = shift(1 + i, s, tot, slot)
            start(move)
            wait_recv(move)
            if i == 0:
                send_second()

            def again(n, c):
                step_of(slot, wc, None)
                return c

            lax.fori_loop(0, s, again, 0)
            wait_send(move)
            last = i == len(shifts) - 1

            def add(z):
                for r in range(rows):
                    v = tot[z + 1, r] + slot[z + 1, r]
                    if last:
                        anc[z + 1, r] = v + natural(gue, z, r)
                    else:
                        tot[z + 1, r] = v

            planes_loop(add)
        for d in range(1, ns):
            start(anchor_copy(d, lax.rem(h + d, ns)))

    @pl.when(jnp.logical_not(active))
    def _():
        for a in second:
            arrive(a)
        weights()
        for d in range(1, ns):
            @pl.when(lax.rem(h + ns - d, ns) == owner)
            def _():
                wait_recv(anchor_copy(d, h))

    @pl.when(active)
    def _():
        for d in range(1, ns):
            wait_send(anchor_copy(d, lax.rem(h + d, ns)))

    results = []
    for j in range(cf):
        if j > 0:
            step_of(anc, wf, src.at[j])

        def put(z, c):
            for r in range(rows):
                stage[j, z, pl.ds(r, SUB, stride=rows), :] = anc[h * zl + z + 1, r]
            return c

        lax.fori_loop(0, zl, put, 0)
        copy = pltpu.make_async_copy(stage.at[j], out.at[j], out_sem.at[j])
        copy.start()
        results.append(copy)
    for d in range(1, ns):
        target = lax.rem(h + d, ns)

        @pl.when(target == owner)
        def _():
            for a in first[-2:]:
                piece(a, d, h, target).wait_send()

        @pl.when(target != owner)
        def _():
            for a in second:
                piece(a, d, h, target).wait_send()
    for copy in results:
        copy.wait()


def per_device(nt, ns, forcing, conductivity, guess):
    cf, zl, sx, sy = forcing.shape
    nz = zl * ns
    rows = sx // SUB
    hops = max(1, (nt - 1).bit_length())
    f32 = jnp.float32
    field = pltpu.VMEM((nz + 2, rows, SUB, sy), f32)
    inner = pltpu.VMEM((nz, rows, SUB, sy), f32)
    plain = pltpu.VMEM((nz, sx, sy), f32)
    dma = pltpu.SemaphoreType.DMA
    return pl.pallas_call(
        functools.partial(kernel, nt, ns, cf, zl, sx),
        out_shape=jax.ShapeDtypeStruct(forcing.shape, f32),
        in_specs=[pl.BlockSpec(memory_space=pl.ANY)] * 3,
        out_specs=pl.BlockSpec(memory_space=pl.ANY),
        scratch_shapes=[
            plain, plain, pltpu.VMEM((cf, nz, sx, sy), f32),
            field, field, field, field, field,
            pltpu.VMEM((hops, nz + 2, rows, SUB, sy), f32),
            inner, inner, inner,
            pltpu.VMEM((cf, zl, sx, sy), f32),
            dma((cf + 2,)), dma((cf + 2, ns)), dma((cf + 2, ns)),
            dma((hops + 1, PARTS)), dma((hops + 1, PARTS)),
            dma((ns, PARTS)), dma((ns, PARTS)), dma((cf,)),
        ],
        compiler_params=pltpu.CompilerParams(
            collective_id=0, has_side_effects=True, vmem_limit_bytes=56 * 1024 * 1024),
    )(forcing, conductivity, guess)


def solution(mesh):
    in_specs = (P("tm", "space", None, None), P("space", None, None), P("tm", "space", None, None))
    return jax.shard_map(
        functools.partial(per_device, mesh.shape["tm"], mesh.shape["space"]),
        mesh=mesh, in_specs=in_specs, out_specs=P("tm", "space", None, None), check_vma=False)
```
